512 devices in a mesh: seq: 128 (over z, x, core), head: 4 (over y).
Axes of the slice: x: 4, y: 4, z: 16, core: 2. Of those that a mesh axis runs over, the one named last changes fastest.
Arguments:
- queries: bfloat16 [32768, 4096], P('seq', 'head'), may hold values from -100 to 100
- keys_values: bfloat16 [32768, 2, 512], P('seq', None, 'head'), may hold values from -4.5 to 4.5
- cache_kv: bfloat16 [32768, 2, 512], P('seq', None, 'head'), may hold values from -4 to 4
- vertical_pages: int32 [4, 4], P('head'), may hold values from 0 to 255, as said below
- slash_shift: int32 [4, 3], P('head'), may hold values from 1 to 128, as said below
- slash_live: int32 [128, 4, 3], P('seq', 'head'), may hold values 0 or 1
- out_proj: bfloat16 [4096, 2048], P('head'), may hold values from -0.09375 to 0.09375
Outputs:
- projected: bfloat16 [32768, 2048], P('seq', 'head')
The draws below stay inside these ranges and needn't reach their ends.
Inputs may be any that keep to these rules, and one draw needn't show every extreme that they name: `vertical_pages`: each head group lists 4 distinct pages. `slash_shift`: each head group lists 3 distinct distances.
All inputs are finite; a program needn't handle non-finite values. No bound on the sum of `slash_live` on one device may be relied on, other than what follows from the above.
Results may differ from the reference program's by a relative error of at most 0.0057.
Values may be sent and summed in bfloat16 or wider, within the bound.
A program may use at most 64 MiB of HBM per device.

```python
import jax
import jax.numpy as jnp
from jax import lax

D = 2048
HEADS = 32
KVH = 4
HD = 128
ROWS = 256
PAGE = 128
VPAGES = 4
SLASH = 3
SHARDS = 128
TOKENS = 32768
PPS = 2
CPAGES = 256


def joint_draw(key):
    query_key = jax.random.fold_in(key, 11)
    pair_key = jax.random.fold_in(key, 12)
    pair_store = jnp.clip(jax.random.normal(pair_key, (TOKENS, 2, KVH * HD), jnp.float32), -4.0, 4.0)
    query_store = jnp.clip(jax.random.normal(query_key, (TOKENS, HEADS * HD), jnp.float32), -4.0, 4.0)
    return (query_store, pair_store)


def draw_queries(key, part):
    return joint_draw(key)[0].astype(jnp.bfloat16)


def draw_keys_values(key, part):
    return joint_draw(key)[1].astype(jnp.bfloat16)


def draw_vertical_pages(key, part):
    group_keys = jax.random.split(jax.random.fold_in(key, 21), KVH)
    chosen = jax.vmap(lambda group_key: jax.random.permutation(group_key, CPAGES)[:VPAGES])(group_keys)
    return chosen.astype(jnp.int32)


def draw_slash_shift(key, part):
    group_keys = jax.random.split(jax.random.fold_in(key, 31), KVH)
    chosen = jax.vmap(lambda group_key: jax.random.permutation(group_key, SHARDS)[:SLASH] + 1)(group_keys)
    return chosen.astype(jnp.int32)


def set_ends(drawn, rng, least, largest):
    spot = [jax.random.randint(jax.random.fold_in(rng, axis), (), 0, length) for axis, length in enumerate(drawn.shape)]
    widest = drawn.shape.index(max(drawn.shape))
    beside = spot[:widest] + [(spot[widest] + 1) % drawn.shape[widest]] + spot[widest + 1:]
    return drawn.at[tuple(spot)].set(least).at[tuple(beside)].set(largest)


def steps_of(stream_key, shape, cuts, least, largest):
    def one(axis_at, shards_of):
        heights = jax.random.uniform(jax.random.fold_in(jax.random.fold_in(stream_key, 6), axis_at), (shards_of,), jnp.float32, least / len(cuts), largest / len(cuts))
        return jnp.repeat(jnp.exp(heights), shape[axis_at] // shards_of).reshape((-1,) + (1,) * (len(shape) - axis_at - 1))

    level = one(*cuts[0])
    for cut in cuts[1:]:
        level = level * one(*cut)
    return level


def normal_values(rng, extent, spread, reach, shards=(), kind=jnp.bfloat16):
    gain = steps_of(rng, extent, shards, -0.22, 0.18) if shards else 1.0
    drawn = jax.random.normal(rng, extent, jnp.float32) * spread * gain
    return jnp.minimum(jnp.maximum(drawn, -reach), reach).astype(kind)


def setup_inputs(seed: int = 0) -> dict:
    splits = jax.random.split(jax.random.key(seed), 8)
    queries = draw_queries(jax.random.fold_in(splits[7], 71), 0)
    keys_values = draw_keys_values(jax.random.fold_in(splits[7], 71), 0)
    cache_kv = normal_values(splits[2], (TOKENS, 2, KVH * HD), 1.0, 4.0, ((0, 128), (2, 4)))
    vertical_pages = draw_vertical_pages(jax.random.fold_in(splits[7], 71), 0)
    slash_shift = draw_slash_shift(jax.random.fold_in(splits[7], 71), 0)
    slash_live = set_ends((jax.random.randint(splits[5], (SHARDS, KVH, SLASH), 0, 4) < 3).astype(jnp.int32), jax.random.fold_in(splits[5], 1), 0, 1)
    out_proj = normal_values(splits[6], (HEADS * HD, D), (HEADS * HD) ** -0.5, 0.09375, ((0, 4),))
    return dict(queries=queries, keys_values=keys_values, cache_kv=cache_kv, vertical_pages=vertical_pages, slash_shift=slash_shift, slash_live=slash_live, out_proj=out_proj)


def reference(queries, keys_values, cache_kv, vertical_pages, slash_shift, slash_live, out_proj):
    group_heads = HEADS // KVH
    all_store = jnp.concatenate([cache_kv, keys_values], 0)

    def one_shard(shard_index):
        start_row = shard_index * ROWS
        query_block = lax.dynamic_slice_in_dim(queries, start_row, ROWS, 0).astype(jnp.float32)
        query_block = query_block.reshape(ROWS, KVH, group_heads, HD)
        local_block = lax.dynamic_slice_in_dim(keys_values, start_row, ROWS, 0)
        row_ids = lax.broadcasted_iota(jnp.int32, (ROWS, ROWS), 0)
        col_ids = lax.broadcasted_iota(jnp.int32, (ROWS, ROWS), 1)
        causal = row_ids >= col_ids
        group_outputs = []
        for group_index in range(KVH):
            low_col = group_index * HD
            high_col = low_col + HD
            distances = slash_shift[group_index]
            key_shards = (SHARDS + shard_index - distances).astype(jnp.int32)
            slash_block = jax.vmap(lambda shard_key: lax.dynamic_slice_in_dim(all_store, shard_key * ROWS, ROWS, 0))(key_shards)
            slash_block = slash_block[:, :, :, low_col:high_col].reshape(SLASH * ROWS, 2, HD)
            page_ids = vertical_pages[group_index]
            page_block = jax.vmap(lambda page_key: lax.dynamic_slice_in_dim(cache_kv, page_key * PAGE, PAGE, 0))(page_ids)
            page_block = page_block[:, :, :, low_col:high_col].reshape(VPAGES * PAGE, 2, HD)
            live_blocks = slash_live[shard_index, group_index] == 1
            clash = live_blocks[None, :] & (distances[None, :] > shard_index) & ((page_ids // PPS)[:, None] == key_shards[None, :])
            page_open = jnp.logical_not(jnp.any(clash, axis=1))
            column_open = jnp.concatenate([jnp.repeat(live_blocks, ROWS), jnp.repeat(page_open, PAGE)])
            visible = jnp.concatenate([causal, jnp.broadcast_to(column_open[None, :], (ROWS, column_open.shape[0]))], 1)
            all_keys = jnp.concatenate([local_block[:, :, low_col:high_col], slash_block, page_block], 0).astype(jnp.float32)
            scores = jnp.einsum("rgd,kd->grk", query_block[:, group_index], all_keys[:, 0, :]) * (HD ** -0.5)
            scores = jnp.where(visible[None], scores, -jnp.inf)
            row_max = jnp.max(scores, axis=2, keepdims=True)
            weights = jnp.exp(scores - row_max)
            row_total = jnp.sum(weights, axis=2, keepdims=True)
            weights_bf = (weights / row_total).astype(jnp.bfloat16).astype(jnp.float32)
            attended = jnp.einsum("grk,kd->rgd", weights_bf, all_keys[:, 1, :]).astype(jnp.bfloat16)
            group_outputs.append(attended)
        attended_all = jnp.stack(group_outputs, 1).reshape(ROWS, HEADS * HD)
        return jnp.dot(attended_all, out_proj, preferred_element_type=jnp.float32).astype(jnp.bfloat16)

    blocks = lax.map(one_shard, jnp.arange(SHARDS, dtype=jnp.int32))
    return blocks.reshape(TOKENS, D)
```

```python
import functools

import jax
import jax.numpy as jnp
from jax import lax
from jax.experimental import pallas as pl
from jax.experimental.pallas import tpu as pltpu
from jax.sharding import PartitionSpec as P

MESH = pl.DeviceIdType.MESH
NC = 4
NZ, NX = 16, 4
CR = 32
KC = 3 * 2 * CR + 4 * CR
NEG = -1e30


def place():
    s = lax.axis_index("seq")
    return s // 8, (s // 2) % NX, s % 2, lax.axis_index("head")


def at(z, x, c, y):
    return (lax.rem(z + NZ, NZ) * 8 + lax.rem(x + NX, NX) * 2 + lax.rem(c + 2, 2), y)


def fetch_kernel(shift, pages, src, out, *scratch):
    zb, xb = scratch[:NC], scratch[NC : 2 * NC]
    sel, cs, cr = (scratch[2 * NC + NC * i : 2 * NC + NC * (i + 1)] for i in range(3))
    zsend, zrecv, xsend, xrecv = scratch[5 * NC :]
    z, x, c, y = place()
    j = x * 2 + c
    up, down = at(z + 1, x, c, y), at(z - 1, x, c, y)
    right, left = at(z, x + 1, c, y), at(z, x - 1, c, y)
    twin = at(z, x, 1 - c, y)

    bar = pltpu.get_barrier_semaphore()
    for peer in (up, down, right, left, twin):
        pl.semaphore_signal(bar, inc=1, device_id=peer, device_id_type=MESH)
    for ch in range(NC):
        zb[ch][z] = src[ch]
    pl.semaphore_wait(bar, 5)

    started = []

    def zcopy(ch, way, hop):
        block = lax.rem(z + NZ - hop, NZ) if way == 0 else lax.rem(z + hop, NZ)
        view = zb[ch].at[block] if hop < 7 else zb[ch].at[block, way]
        return pltpu.make_async_remote_copy(
            src_ref=view, dst_ref=view,
            send_sem=zsend.at[ch, way, hop], recv_sem=zrecv.at[ch, way, hop],
            device_id=up if way == 0 else down, device_id_type=MESH,
        )

    def zarrive(ch, way, hop):
        block = lax.rem(z + NZ - hop - 1, NZ) if way == 0 else lax.rem(z + hop + 1, NZ)
        view = zb[ch].at[block] if hop < 7 else zb[ch].at[block, way]
        pltpu.make_async_remote_copy(
            src_ref=view, dst_ref=view,
            send_sem=zsend.at[ch, way, hop], recv_sem=zrecv.at[ch, way, hop],
            device_id=up if way == 0 else down, device_id_type=MESH,
        ).wait_recv()

    def zstep(ch, hop):
        for way in range(2):
            if hop > 0:
                zarrive(ch, way, hop - 1)
            cp = zcopy(ch, way, hop)
            cp.start()
            started.append(cp)

    def send(ch, slot, view, dst, to):
        cp = pltpu.make_async_remote_copy(
            src_ref=view, dst_ref=dst, send_sem=xsend.at[ch, slot], recv_sem=xrecv.at[ch, slot],
            device_id=to, device_id_type=MESH,
        )
        cp.start()
        started.append(cp)

    def arrive(ch, slot, dst, to):
        pltpu.make_async_remote_copy(
            src_ref=dst, dst_ref=dst, send_sem=xsend.at[ch, slot], recv_sem=xrecv.at[ch, slot],
            device_id=to, device_id_type=MESH,
        ).wait_recv()

    def xstep(ch, step):
        xl, xr, xo = lax.rem(x + 3, NX), lax.rem(x + 1, NX), lax.rem(x + 2, NX)
        if step == 0:
            for way in range(2):
                zarrive(ch, way, 7)
            for k in range(3):
                d = shift[0, k]
                r, q = lax.rem(d, 8), d // 8
                m = q + jnp.where(j + r >= 8, 1, 0)
                from_slab = z - m >= 0
                zs = lax.rem(z - m + 2 * NZ, NZ)
                got = zb[ch][zs, jnp.where(from_slab, 0, 1)]
                sel[ch][k * 2 * CR : (k + 1) * 2 * CR] = got[0].reshape(2 * CR, 128)
                sel[ch][KC + k * 2 * CR : KC + (k + 1) * 2 * CR] = got[1].reshape(2 * CR, 128)
            for i in range(4):
                p = pages[0, i]
                got = zb[ch][p // 16, 1, :, lax.rem(p, 2)]
                lo = 6 * CR + i * CR
                sel[ch][lo : lo + CR] = got[0]
                sel[ch][KC + lo : KC + lo + CR] = got[1]
            xb[ch][x] = sel[ch][...]
            send(ch, 0, sel[ch], xb[ch].at[x], right)
            send(ch, 1, sel[ch], xb[ch].at[x], left)
        if step == 1:
            arrive(ch, 0, xb[ch].at[xl], right)
            lo = xb[ch].at[xl, pl.ds(0, KC)]
            send(ch, 2, lo, lo, right)
            arrive(ch, 1, xb[ch].at[xr], left)
            hi = xb[ch].at[xr, pl.ds(KC, KC)]
            send(ch, 3, hi, hi, left)
        if step == 2:
            arrive(ch, 2, xb[ch].at[xo, pl.ds(0, KC)], right)
            arrive(ch, 3, xb[ch].at[xo, pl.ds(KC, KC)], left)
            for who, put in ((j, out.at[ch]), (lax.rem(j + 1, 2) + (j // 2) * 2, cs[ch])):
                for k in range(3):
                    r = lax.rem(shift[0, k], 8)
                    xs = lax.rem(who - r + 8, 8) // 2
                    for half in range(2):
                        lo = half * KC + k * 2 * CR
                        put[lo : lo + 2 * CR] = xb[ch][xs, lo : lo + 2 * CR]
                for i in range(4):
                    xs = lax.rem(pages[0, i] // 2, 8) // 2
                    for half in range(2):
                        lo = half * KC + 6 * CR + i * CR
                        put[lo : lo + CR] = xb[ch][xs, lo : lo + CR]
            send(ch, 4, cs[ch], cr[ch], twin)
        if step == 3:
            arrive(ch, 4, cr[ch], twin)
            for k in range(3):
                r = lax.rem(shift[0, k], 8)
                mine = lax.rem(lax.rem(j - r + 8, 8), 2) == c
                for half in range(2):
                    lo = half * KC + k * 2 * CR
                    out[ch, lo : lo + 2 * CR] = jnp.where(
                        mine, out[ch, lo : lo + 2 * CR], cr[ch][lo : lo + 2 * CR]
                    )
            for i in range(4):
                mine = lax.rem(pages[0, i] // 2, 2) == c
                for half in range(2):
                    lo = half * KC + 6 * CR + i * CR
                    out[ch, lo : lo + CR] = jnp.where(
                        mine, out[ch, lo : lo + CR], cr[ch][lo : lo + CR]
                    )

    for hop in range(8):
        for ch in (0, 1):
            zstep(ch, hop)
    for hop in range(8):
        for ch in (2, 3):
            zstep(ch, hop)
        if hop in (0, 2, 4, 6):
            xstep(0, hop // 2)
        if hop in (1, 3, 5, 7):
            xstep(1, hop // 2)
    for step in range(4):
        for ch in (2, 3):
            xstep(ch, step)
    for cp in started:
        cp.wait_send()


def fetch(shift, pages, src):
    smem = pl.BlockSpec(memory_space=pltpu.SMEM)
    vmem = pl.BlockSpec(memory_space=pltpu.VMEM)
    bf = jnp.bfloat16
    return pl.pallas_call(
        fetch_kernel,
        name="fetch",
        out_shape=jax.ShapeDtypeStruct((NC, 2 * KC, 128), bf),
        in_specs=[smem, smem, vmem],
        out_specs=vmem,
        scratch_shapes=[pltpu.VMEM((NZ, 2, 2, 2, CR, 128), bf)] * NC
        + [pltpu.VMEM((NX, 2 * KC, 128), bf)] * NC
        + [pltpu.VMEM((2 * KC, 128), bf)] * (3 * NC)
        + [pltpu.SemaphoreType.DMA((NC, 2, 8))] * 2
        + [pltpu.SemaphoreType.DMA((NC, 5))] * 2,
        compiler_params=pltpu.CompilerParams(
            collective_id=0, has_side_effects=True, vmem_limit_bytes=48 * 2**20
        ),
    )(shift, pages, src)


def attend_kernel(shift, pages, live, q, src, got, att):
    s = lax.axis_index("seq")
    own = NC * 2 * CR
    scale = 128**-0.5 * 1.4426950408889634
    rows = lax.broadcasted_iota(jnp.int32, (own, own), 0)
    at_ = lax.broadcasted_iota(jnp.int32, (own, own), 1)
    cols = (at_ // CR) % 2 * 128 + at_ // (2 * CR) * CR + at_ % CR
    causal = rows >= cols
    lane = lax.broadcasted_iota(jnp.int32, (1, KC), 1)
    bias = jnp.zeros((1, KC), jnp.float32)
    for k in range(3):
        here = (lane >= k * 2 * CR) & (lane < (k + 1) * 2 * CR)
        bias = jnp.where(here & (live[0, k] != 1), NEG, bias)
    for i in range(4):
        shut = False
        for k in range(3):
            d = shift[0, k]
            shut = shut | ((live[0, k] == 1) & (d > s) & (s + 128 - d == pages[0, i] // 2))
        here = (lane >= 6 * CR + i * CR) & (lane < 6 * CR + (i + 1) * CR)
        bias = jnp.where(here & shut, NEG, bias)
    bias = jnp.concatenate([bias] * NC, 1)
    keys0 = jnp.concatenate([src[ch, 0, 0].reshape(2 * CR, 128) for ch in range(NC)], 0)
    vals0 = jnp.concatenate([src[ch, 0, 1].reshape(2 * CR, 128) for ch in range(NC)], 0)
    keys1 = jnp.concatenate([got[ch, :KC] for ch in range(NC)], 0)
    vals1 = jnp.concatenate([got[ch, KC:] for ch in range(NC)], 0)
    contract = (((1,), (1,)), ((), ()))
    for h in range(8):
        qh = q[:, h * 128 : (h + 1) * 128]
        s0 = lax.dot_general(qh, keys0, contract, preferred_element_type=jnp.float32)
        s1 = lax.dot_general(qh, keys1, contract, preferred_element_type=jnp.float32)
        s0 = jnp.where(causal, s0, NEG)
        s1 = s1 + bias
        top = jnp.maximum(jnp.max(s0, 1, keepdims=True), jnp.max(s1, 1, keepdims=True))
        e0 = jnp.exp2((s0 - top) * scale)
        e1 = jnp.exp2((s1 - top) * scale)
        total = jnp.sum(e0, 1, keepdims=True) + jnp.sum(e1, 1, keepdims=True)
        o = jnp.dot(e0.astype(jnp.bfloat16), vals0, preferred_element_type=jnp.float32)
        o += jnp.dot(e1.astype(jnp.bfloat16), vals1, preferred_element_type=jnp.float32)
        att[:, h * 128 : (h + 1) * 128] = (o / total).astype(jnp.bfloat16)


def attend(shift, pages, live, q, src, got):
    smem = pl.BlockSpec(memory_space=pltpu.SMEM)
    vmem = pl.BlockSpec(memory_space=pltpu.VMEM)
    return pl.pallas_call(
        attend_kernel,
        name="attend",
        out_shape=jax.ShapeDtypeStruct(q.shape, jnp.bfloat16),
        in_specs=[smem, smem, smem, vmem, vmem, vmem],
        out_specs=vmem,
        compiler_params=pltpu.CompilerParams(vmem_limit_bytes=48 * 2**20),
    )(shift, pages, live, q, src, got)


def project_kernel(att, w, out, parts, inbox, ssem, rsem):
    s, y = lax.axis_index("seq"), lax.axis_index("head")
    bar = pltpu.get_barrier_semaphore()
    for step in (1, 2, 3):
        pl.semaphore_signal(
            bar, inc=1, device_id=(s, lax.rem(y + step, 4)), device_id_type=MESH
        )
    pl.semaphore_wait(bar, 3)
    a = att[...]
    sends = []
    for step in (2, 1, 3):
        to = lax.rem(y + step, 4)
        cols = pl.ds(pl.multiple_of(to * 512, 512), 512)
        parts[step - 1] = jnp.dot(
            a, w[:, cols], preferred_element_type=jnp.float32
        ).astype(jnp.bfloat16)
        cp = pltpu.make_async_remote_copy(
            src_ref=parts.at[step - 1], dst_ref=inbox.at[step - 1],
            send_sem=ssem.at[step - 1], recv_sem=rsem.at[step - 1],
            device_id=(s, to), device_id_type=MESH,
        )
        cp.start()
        sends.append(cp)
    total = jnp.dot(
        a, w[:, pl.ds(pl.multiple_of(y * 512, 512), 512)], preferred_element_type=jnp.float32
    )
    for cp, step in zip(sends, (2, 1, 3)):
        cp.wait()
    out[...] = (
        total + inbox[0].astype(jnp.float32) + inbox[1].astype(jnp.float32)
        + inbox[2].astype(jnp.float32)
    ).astype(jnp.bfloat16)


def project(att, w):
    vmem = pl.BlockSpec(memory_space=pltpu.VMEM)
    return pl.pallas_call(
        project_kernel,
        name="project",
        out_shape=jax.ShapeDtypeStruct((att.shape[0], 512), jnp.bfloat16),
        in_specs=[vmem, vmem],
        out_specs=vmem,
        scratch_shapes=[
            pltpu.VMEM((3, att.shape[0], 512), jnp.bfloat16),
            pltpu.VMEM((3, att.shape[0], 512), jnp.bfloat16),
            pltpu.SemaphoreType.DMA((3,)),
            pltpu.SemaphoreType.DMA((3,)),
        ],
        compiler_params=pltpu.CompilerParams(
            collective_id=1, has_side_effects=True, vmem_limit_bytes=48 * 2**20
        ),
    )(att, w)


def chunked(kv):
    return kv.reshape(2, NC, CR, 2, 128).transpose(1, 3, 0, 2, 4)


def body(queries, keys_values, cache_kv, vertical_pages, slash_shift, slash_live, out_proj):
    src = jnp.stack([chunked(keys_values), chunked(cache_kv)], 1)
    got = fetch(slash_shift, vertical_pages, src)
    att = attend(slash_shift, vertical_pages, slash_live[0], queries, src, got)
    return project(att, out_proj)


def solution(mesh):
    placed = (
        P("seq", "head"),
        P("seq", None, "head"),
        P("seq", None, "head"),
        P("head", None),
        P("head", None),
        P("seq", "head", None),
        P("head", None),
    )
    return jax.shard_map(
        body, mesh=mesh, in_specs=placed, out_specs=P("seq", "head"), check_vma=False
    )
```

```python
import functools

import jax
import jax.numpy as jnp
from jax import lax
from jax.experimental import pallas as pl
from jax.experimental.pallas import tpu as pltpu
from jax.sharding import PartitionSpec as P

MESH = pl.DeviceIdType.MESH
NC = 4
NZ, NX = 16, 4
NT = 4
CR = 32
KC = 3 * 2 * CR + 4 * CR
NEG = -1e30


def place():
    s = lax.axis_index("seq")
    return s // 8, (s // 2) % NX, s % 2, lax.axis_index("head")


def at(z, x, c, y):
    return (lax.rem(z + NZ, NZ) * 8 + lax.rem(x + NX, NX) * 2 + lax.rem(c + 2, 2), y)


SK = 3 * 2 * CR
PK = 4 * CR


def kernel(shift, pages, live, slab, cache, q_hbm, w_hbm, out, *scratch):
    zb = scratch[:NC]
    sel, tw, my, msg_l, fwd_r, fwd_l, a_l, a_r, b_l, b_r = (
        scratch[NC * (i + 1) : NC * (i + 2)] for i in range(10)
    )
    (psel, ptw, pg, pa_l, pa_r, pb_l, pb_r, pcol, pcol2,
     q, w, kall, vall, att, parts, inbox,
     zsend, zrecv, xsend, xrecv, psend, precv, ysend, yrecv, lsem) = scratch[11 * NC :]
    s = lax.axis_index("seq")
    z, x, c, y = place()
    j = x * 2 + c
    up, down = at(z + 1, x, c, y), at(z - 1, x, c, y)
    right, left = at(z, x + 1, c, y), at(z, x - 1, c, y)
    twin = at(z, x, 1 - c, y)

    bar = pltpu.get_barrier_semaphore()
    others = [(s, lax.rem(y + step, 4)) for step in (1, 2, 3)]
    up2, down2 = at(z + 2, x, c, y), at(z - 2, x, c, y)
    for peer in [up, down, down2, right, left, twin] + others:
        pl.semaphore_signal(bar, inc=1, device_id=peer, device_id_type=MESH)
    local = [
        pltpu.make_async_copy(q_hbm, q, lsem.at[0]),
        pltpu.make_async_copy(w_hbm, w, lsem.at[1]),
    ]
    for ch in range(NC):
        zb[ch][z, 0] = slab[ch].reshape(4 * CR, 128)
        zb[ch][z, 1] = cache[ch].reshape(4 * CR, 128)
    pl.semaphore_wait(bar, 9)

    started = []

    def zcopy(ch, way, hop, block):
        view = zb[ch].at[block] if hop < 7 else zb[ch].at[block, way]
        return pltpu.make_async_remote_copy(
            src_ref=view, dst_ref=view,
            send_sem=zsend.at[ch, way, hop], recv_sem=zrecv.at[ch, way, hop],
            device_id=up if way == 0 else down, device_id_type=MESH,
        )

    def zarrive(ch, way, hop):
        block = lax.rem(z + NZ - hop - 1, NZ) if way == 0 else lax.rem(z + hop + 1, NZ)
        zcopy(ch, way, hop, block).wait_recv()

    def zstep(ch, hop):
        for way in range(2):
            if hop > 0:
                zarrive(ch, way, hop - 1)
            block = lax.rem(z + NZ - hop, NZ) if way == 0 else lax.rem(z + hop, NZ)
            cp = zcopy(ch, way, hop, block)
            cp.start()
            started.append(cp)

    def xcopy(ch, slot, view, dst, to):
        return pltpu.make_async_remote_copy(
            src_ref=view, dst_ref=dst, send_sem=xsend.at[ch, slot], recv_sem=xrecv.at[ch, slot],
            device_id=to, device_id_type=MESH,
        )

    def send(ch, slot, view, dst, to):
        cp = xcopy(ch, slot, view, dst, to)
        cp.start()
        started.append(cp)

    def arrive(ch, slot, dst, to):
        xcopy(ch, slot, dst, dst, to).wait_recv()

    def turn(k):
        r = lax.rem(shift[0, k], 8)
        swap = lax.rem(r, 2) == 1
        rho = lax.rem(r // 2 + jnp.where(swap & (c == 0), 1, 0), NX)
        return rho, swap

    def xstep(ch, step):
        if step == 0:
            for way in range(2):
                zarrive(ch, way, 7)
            for k in range(3):
                d = shift[0, k]
                m = d // 8 + jnp.where(j + lax.rem(d, 8) >= 8, 1, 0)
                zs = lax.rem(z - m + 2 * NZ, NZ)
                got = zb[ch][zs, jnp.where(z - m >= 0, 0, 1)]
                for half in range(2):
                    sel[ch][half, k * 2 * CR : (k + 1) * 2 * CR] = got[half * 2 * CR : (half + 1) * 2 * CR]
            send(ch, 0, sel[ch], tw[ch], twin)
        if step == 1:
            arrive(ch, 0, tw[ch], twin)
            for k in range(3):
                rho, swap = turn(k)
                rows = slice(k * 2 * CR, (k + 1) * 2 * CR)
                for half in range(2):
                    my[ch][half, rows] = jnp.where(swap, tw[ch][half, rows], sel[ch][half, rows])
                msg_l[ch][rows] = jnp.where(rho == 2, my[ch][1, rows], my[ch][0, rows])
            send(ch, 1, my[ch].at[0], a_l[ch], right)
            send(ch, 2, msg_l[ch], a_r[ch], left)
        if step == 2:
            arrive(ch, 1, a_l[ch], right)
            arrive(ch, 2, a_r[ch], left)
            for k in range(3):
                rho, _ = turn(k)
                rows = slice(k * 2 * CR, (k + 1) * 2 * CR)
                fwd_r[ch][rows] = jnp.where(rho == 2, a_l[ch][rows], my[ch][1, rows])
                fwd_l[ch][rows] = jnp.where(rho == 2, a_r[ch][rows], my[ch][1, rows])
            send(ch, 3, fwd_r[ch], b_l[ch], right)
            send(ch, 4, fwd_l[ch], b_r[ch], left)
        if step == 3:
            arrive(ch, 3, b_l[ch], right)
            arrive(ch, 4, b_r[ch], left)
            for k in range(3):
                rho, _ = turn(k)
                rows = slice(k * 2 * CR, (k + 1) * 2 * CR)
                lo = ch * SK + k * 2 * CR
                kall[lo : lo + 2 * CR] = jnp.where(
                    rho == 0, my[ch][0, rows],
                    jnp.where(rho == 1, a_l[ch][rows], jnp.where(rho == 2, b_l[ch][rows], a_r[ch][rows])),
                )
                vall[lo : lo + 2 * CR, :128] = jnp.where(
                    rho == 0, my[ch][1, rows], jnp.where(rho == 1, b_l[ch][rows], b_r[ch][rows])
                )

    zc = lax.rem(z, NC)

    def pcopy(slot, view, dst, to):
        return pltpu.make_async_remote_copy(
            src_ref=view, dst_ref=dst, send_sem=psend.at[slot], recv_sem=precv.at[slot],
            device_id=to, device_id_type=MESH,
        )

    def psent(slot, view, dst, to):
        cp = pcopy(slot, view, dst, to)
        cp.start()
        started.append(cp)

    def parrive(slot, dst, to):
        pcopy(slot, dst, dst, to).wait_recv()

    def pstep(step):
        if step == 0:
            for i in range(4):
                p = pages[0, i]
                got = zb[0][p // 16, 1]
                for ch in range(1, NC):
                    got = jnp.where(zc == ch, zb[ch][p // 16, 1], got)
                for half in range(2):
                    lo = half * 2 * CR
                    psel[half, i * CR : (i + 1) * CR] = jnp.where(
                        lax.rem(p, 2) == 0, got[lo : lo + CR], got[lo + CR : lo + 2 * CR]
                    )
            psent(0, psel, ptw, twin)
        if step == 1:
            parrive(0, ptw, twin)
            for i in range(4):
                mine = lax.rem(pages[0, i] // 2, 2) == c
                rows = slice(i * CR, (i + 1) * CR)
                keys_i = jnp.where(mine, psel[0, rows], ptw[0, rows])
                vals_i = jnp.where(mine, psel[1, rows], ptw[1, rows])
                pg[rows] = jnp.where(c == 0, keys_i, vals_i)
            psent(1, pg, pa_l, right)
            psent(2, pg, pa_r, left)
        if step == 2:
            parrive(1, pa_l, right)
            parrive(2, pa_r, left)
            psent(3, pa_l.at[pl.ds(0, PK // 2)], pb_l, right)
            psent(4, pa_r.at[pl.ds(PK // 2, PK // 2)], pb_r, left)
        if step == 3:
            parrive(3, pb_l, right)
            parrive(4, pb_r, left)
            for i in range(4):
                far = lax.rem(lax.rem(pages[0, i] // 4, NX) - x + NX, NX)
                rows = slice(i * CR, (i + 1) * CR)
                opposite = (pb_l if i < 2 else pb_r)[i % 2 * CR : (i % 2 + 1) * CR]
                pcol[zc, rows] = jnp.where(
                    far == 0, pg[rows],
                    jnp.where(far == 3, pa_l[rows], jnp.where(far == 1, pa_r[rows], opposite)),
                )
            psent(5, pcol.at[zc], pcol.at[zc], up)
            psent(6, pcol.at[zc], pcol.at[zc], down)
            psent(7, pcol.at[zc], pcol.at[zc], up2)
        if step == 4:
            parrive(5, pcol.at[lax.rem(zc + 3, NC)], up)
            parrive(6, pcol.at[lax.rem(zc + 1, NC)], down)
            parrive(7, pcol.at[lax.rem(zc + 2, NC)], up2)
            psent(8, pcol, pcol2, twin)
        if step == 5:
            parrive(8, pcol2, twin)
            for ch in range(NC):
                lo = NC * SK + ch * PK
                kall[lo : lo + PK] = jnp.where(c == 0, pcol[ch], pcol2[ch])
                vall[lo : lo + PK, :128] = jnp.where(c == 0, pcol2[ch], pcol[ch])

    for hop in range(8):
        for ch in range(NC):
            zstep(ch, hop)
        if hop == 0:
            for cp in local:
                cp.start()
        if hop == 1:
            vall[:, 128:] = jnp.ones((NC * KC + NC * 2 * CR, 128), jnp.bfloat16)
            for ch in range(NC):
                lo = NC * KC + ch * 2 * CR
                kall[lo : lo + 2 * CR] = slab[ch, 0].reshape(2 * CR, 128)
                vall[lo : lo + 2 * CR, :128] = slab[ch, 1].reshape(2 * CR, 128)
        if hop == 4:
            for cp in local:
                cp.wait()
    for ch in range(NC):
        xstep(ch, 0)
    pstep(0)
    for step in (1, 2, 3):
        for ch in range(NC):
            xstep(ch, step)
            if ch == 0:
                pstep(step)
            if step == 3 and ch == 2:
                pstep(4)
    pstep(5)

    own = NC * 2 * CR
    rows_t = own // NT
    scale = 128**-0.5 * 1.4426950408889634
    lane = lax.broadcasted_iota(jnp.int32, (1, NC * KC), 1)
    bias = jnp.zeros((1, NC * KC), jnp.float32)
    for k in range(3):
        here = (lane < NC * SK) & (lane % SK // (2 * CR) == k)
        bias = jnp.where(here & (live[0, k] != 1), NEG, bias)
    for i in range(4):
        shut = False
        for k in range(3):
            d = shift[0, k]
            shut = shut | ((live[0, k] == 1) & (d > s) & (s + 128 - d == pages[0, i] // 2))
        here = (lane >= NC * SK) & ((lane - NC * SK) % PK // CR == i)
        bias = jnp.where(here & shut, NEG, bias)
    spot = lax.broadcasted_iota(jnp.int32, (rows_t, own), 1)
    cols = (spot // CR) % 2 * 128 + spot // (2 * CR) * CR + spot % CR
    line = lax.broadcasted_iota(jnp.int32, (rows_t, own), 0)

    contract = (((1,), (1,)), ((), ()))
    far = NC * KC
    own_parts = []

    def ycopy(t, step):
        lines = pl.ds(t * rows_t, rows_t)
        return pltpu.make_async_remote_copy(
            src_ref=parts.at[step - 1, lines], dst_ref=inbox.at[step - 1, lines],
            send_sem=ysend.at[t, step - 1], recv_sem=yrecv.at[t, step - 1],
            device_id=(s, lax.rem(y + step, 4)), device_id_type=MESH,
        )

    for t in range(NT):
        lines = slice(t * rows_t, (t + 1) * rows_t)
        qt = jnp.concatenate([q[lines, h * 128 : (h + 1) * 128] for h in range(8)], 0)
        s1 = lax.dot_general(qt, kall[:far], contract, preferred_element_type=jnp.float32)
        s0 = lax.dot_general(qt, kall[far:], contract, preferred_element_type=jnp.float32)
        s1 = s1 + bias
        open_ = jnp.where(line + t * rows_t >= cols, 0.0, NEG)
        s0 = s0 + jnp.concatenate([open_] * 8, 0)
        top = jnp.maximum(jnp.max(s0, 1, keepdims=True), jnp.max(s1, 1, keepdims=True))
        e0 = jnp.exp2((s0 - top) * scale)
        e1 = jnp.exp2((s1 - top) * scale)
        o = jnp.dot(e1.astype(jnp.bfloat16), vall[:far], preferred_element_type=jnp.float32)
        o += jnp.dot(e0.astype(jnp.bfloat16), vall[far:], preferred_element_type=jnp.float32)
        o = (o[:, :128] / o[:, 128:]).astype(jnp.bfloat16)
        for h in range(8):
            att[lines, h * 128 : (h + 1) * 128] = o[h * rows_t : (h + 1) * rows_t]
        a = att[lines]
        for step in (2, 1, 3, 0):
            cols_y = pl.ds(pl.multiple_of(lax.rem(y + step, 4) * 512, 512), 512)
            term = jnp.dot(a, w[:, cols_y], preferred_element_type=jnp.float32)
            if step:
                parts[step - 1, lines] = term.astype(jnp.bfloat16)
                cp = ycopy(t, step)
                cp.start()
                started.append(cp)
            else:
                own_parts.append(term)
    for t in range(NT):
        lines = slice(t * rows_t, (t + 1) * rows_t)
        total = own_parts[t]
        for step in (1, 3, 2):
            ycopy(t, step).wait_recv()
            total = total + inbox[step - 1, lines].astype(jnp.float32)
        out[lines] = total.astype(jnp.bfloat16)
    for cp in started:
        cp.wait_send()


def call(shift, pages, live, slab, cache, q, w):
    smem = pl.BlockSpec(memory_space=pltpu.SMEM)
    vmem = pl.BlockSpec(memory_space=pltpu.VMEM)
    whole = pl.BlockSpec(memory_space=pl.ANY)
    bf, dma = jnp.bfloat16, pltpu.SemaphoreType.DMA
    rows = q.shape[0]
    keys = NC * KC + NC * 2 * CR

    def many(*shape):
        return [pltpu.VMEM(shape, bf)] * NC

    return pl.pallas_call(
        kernel,
        name="attention",
        out_shape=jax.ShapeDtypeStruct((rows, 512), bf),
        in_specs=[smem, smem, smem, vmem, vmem, whole, whole],
        out_specs=vmem,
        scratch_shapes=many(NZ, 2, 4 * CR, 128)
        + many(2, SK, 128) * 3
        + many(SK, 128) * 7
        + [pltpu.VMEM((2, PK, 128), bf)] * 2
        + [pltpu.VMEM((PK, 128), bf)] * 3
        + [pltpu.VMEM((PK // 2, 128), bf)] * 2
        + [pltpu.VMEM((NC, PK, 128), bf)] * 2
        + [
            pltpu.VMEM(q.shape, bf),
            pltpu.VMEM(w.shape, bf),
            pltpu.VMEM((keys, 128), bf),
            pltpu.VMEM((keys, 256), bf),
            pltpu.VMEM(q.shape, bf),
            pltpu.VMEM((3, rows, 512), bf),
            pltpu.VMEM((3, rows, 512), bf),
        ]
        + [dma((NC, 2, 8))] * 2 + [dma((NC, 5))] * 2 + [dma((9,))] * 2 + [dma((NT, 3))] * 2 + [dma((2,))],
        compiler_params=pltpu.CompilerParams(
            collective_id=0, has_side_effects=True, vmem_limit_bytes=56 * 2**20
        ),
    )(shift, pages, live, slab, cache, q, w)


def chunked(kv):
    return kv.reshape(2, NC, CR, 2, 128).transpose(1, 3, 0, 2, 4)


def body(queries, keys_values, cache_kv, vertical_pages, slash_shift, slash_live, out_proj):
    return call(
        slash_shift, vertical_pages, slash_live[0], chunked(keys_values), chunked(cache_kv), queries, out_proj
    )


def solution(mesh):
    placed = (
        P("seq", "head"),
        P("seq", None, "head"),
        P("seq", None, "head"),
        P("head", None),
        P("head", None),
        P("seq", "head", None),
        P("head", None),
    )
    return jax.shard_map(
        body, mesh=mesh, in_specs=placed, out_specs=P("seq", "head"), check_vma=False
    )
```

```python
import functools

import jax
import jax.numpy as jnp
from jax import lax
from jax.experimental import pallas as pl
from jax.experimental.pallas import tpu as pltpu
from jax.sharding import PartitionSpec as P

MESH = pl.DeviceIdType.MESH
NC = 4
NZ, NX = 16, 4
TILES = (96, 96, 64)
NT = len(TILES)
CR = 32
KC = 3 * 2 * CR + 4 * CR
NEG = -1e30


def place():
    s = lax.axis_index("seq")
    return s // 8, (s // 2) % NX, s % 2, lax.axis_index("head")


def at(z, x, c, y):
    return (lax.rem(z + NZ, NZ) * 8 + lax.rem(x + NX, NX) * 2 + lax.rem(c + 2, 2), y)


SK = 3 * 2 * CR
PK = 4 * CR


def kernel(shift, pages, live, slab, cache, q_hbm, w_hbm, out, *scratch):
    zb = scratch[:NC]
    sel, tw, my, msg_l, fwd_r, fwd_l, a_l, a_r, b_l, b_r = (
        scratch[NC * (i + 1) : NC * (i + 2)] for i in range(10)
    )
    (psel, ptw, pg, pa_l, pa_r, pb_l, pb_r, pcol, pcol2,
     q, w, qs, kall, vall, att, near, t0, t1, t3,
     p2a, p2b, s1a, s1b, s3a, s3b, hop_l, hop_r, in_la, in_lb, in_ra, in_rb,
     zsend, zrecv, xsend, xrecv, psend, precv, ysend, yrecv, lsem) = scratch[11 * NC :]
    s = lax.axis_index("seq")
    z, x, c, y = place()
    j = x * 2 + c
    up, down = at(z + 1, x, c, y), at(z - 1, x, c, y)
    right, left = at(z, x + 1, c, y), at(z, x - 1, c, y)
    twin = at(z, x, 1 - c, y)

    bar = pltpu.get_barrier_semaphore()
    others = [(s, lax.rem(y + step, 4)) for step in (1, 3)]
    up2, down2 = at(z + 2, x, c, y), at(z - 2, x, c, y)
    for peer in [up, down, down2, right, left, twin] + others:
        pl.semaphore_signal(bar, inc=1, device_id=peer, device_id_type=MESH)
    local = [
        pltpu.make_async_copy(q_hbm, q, lsem.at[0]),
        pltpu.make_async_copy(w_hbm, w, lsem.at[1]),
    ]
    for ch in range(NC):
        zb[ch][z, 0] = slab[ch].reshape(4 * CR, 128)
        zb[ch][z, 1] = cache[ch].reshape(4 * CR, 128)
    pl.semaphore_wait(bar, 8)

    started = []

    def zcopy(ch, way, hop, block):
        view = zb[ch].at[block] if hop < 7 else zb[ch].at[block, way]
        return pltpu.make_async_remote_copy(
            src_ref=view, dst_ref=view,
            send_sem=zsend.at[ch, way, hop], recv_sem=zrecv.at[ch, way, hop],
            device_id=up if way == 0 else down, device_id_type=MESH,
        )

    def zarrive(ch, way, hop):
        block = lax.rem(z + NZ - hop - 1, NZ) if way == 0 else lax.rem(z + hop + 1, NZ)
        zcopy(ch, way, hop, block).wait_recv()

    def zstep(ch, hop):
        for way in range(2):
            if hop > 0:
                zarrive(ch, way, hop - 1)
            block = lax.rem(z + NZ - hop, NZ) if way == 0 else lax.rem(z + hop, NZ)
            cp = zcopy(ch, way, hop, block)
            cp.start()
            started.append(cp)

    def xcopy(ch, slot, view, dst, to):
        return pltpu.make_async_remote_copy(
            src_ref=view, dst_ref=dst, send_sem=xsend.at[ch, slot], recv_sem=xrecv.at[ch, slot],
            device_id=to, device_id_type=MESH,
        )

    def send(ch, slot, view, dst, to):
        cp = xcopy(ch, slot, view, dst, to)
        cp.start()
        started.append(cp)

    def arrive(ch, slot, dst, to):
        xcopy(ch, slot, dst, dst, to).wait_recv()

    def turn(k):
        r = lax.rem(shift[0, k], 8)
        swap = lax.rem(r, 2) == 1
        rho = lax.rem(r // 2 + jnp.where(swap & (c == 0), 1, 0), NX)
        return rho, swap

    def xstep(ch, step):
        if step == 0:
            for way in range(2):
                zarrive(ch, way, 7)
            for k in range(3):
                d = shift[0, k]
                m = d // 8 + jnp.where(j + lax.rem(d, 8) >= 8, 1, 0)
                zs = lax.rem(z - m + 2 * NZ, NZ)
                got = zb[ch][zs, jnp.where(z - m >= 0, 0, 1)]
                for half in range(2):
                    sel[ch][half, k * 2 * CR : (k + 1) * 2 * CR] = got[half * 2 * CR : (half + 1) * 2 * CR]
            send(ch, 0, sel[ch], tw[ch], twin)
        if step == 1:
            arrive(ch, 0, tw[ch], twin)
            for k in range(3):
                rho, swap = turn(k)
                rows = slice(k * 2 * CR, (k + 1) * 2 * CR)
                for half in range(2):
                    my[ch][half, rows] = jnp.where(swap, tw[ch][half, rows], sel[ch][half, rows])
                msg_l[ch][rows] = jnp.where(rho == 2, my[ch][1, rows], my[ch][0, rows])
            send(ch, 1, my[ch].at[0], a_l[ch], right)
            send(ch, 2, msg_l[ch], a_r[ch], left)
        if step == 2:
            arrive(ch, 1, a_l[ch], right)
            arrive(ch, 2, a_r[ch], left)
            for k in range(3):
                rho, _ = turn(k)
                rows = slice(k * 2 * CR, (k + 1) * 2 * CR)
                fwd_r[ch][rows] = jnp.where(rho == 2, a_l[ch][rows], my[ch][1, rows])
                fwd_l[ch][rows] = jnp.where(rho == 2, a_r[ch][rows], my[ch][1, rows])
            send(ch, 3, fwd_r[ch], b_l[ch], right)
            send(ch, 4, fwd_l[ch], b_r[ch], left)
        if step == 3:
            arrive(ch, 3, b_l[ch], right)
            arrive(ch, 4, b_r[ch], left)
            for k in range(3):
                rho, _ = turn(k)
                rows = slice(k * 2 * CR, (k + 1) * 2 * CR)
                lo = ch * SK + k * 2 * CR
                kall[lo : lo + 2 * CR] = jnp.where(
                    rho == 0, my[ch][0, rows],
                    jnp.where(rho == 1, a_l[ch][rows], jnp.where(rho == 2, b_l[ch][rows], a_r[ch][rows])),
                )
                vall[lo : lo + 2 * CR, :128] = jnp.where(
                    rho == 0, my[ch][1, rows], jnp.where(rho == 1, b_l[ch][rows], b_r[ch][rows])
                )

    zc = lax.rem(z, NC)

    def pcopy(slot, view, dst, to):
        return pltpu.make_async_remote_copy(
            src_ref=view, dst_ref=dst, send_sem=psend.at[slot], recv_sem=precv.at[slot],
            device_id=to, device_id_type=MESH,
        )

    def psent(slot, view, dst, to):
        cp = pcopy(slot, view, dst, to)
        cp.start()
        started.append(cp)

    def parrive(slot, dst, to):
        pcopy(slot, dst, dst, to).wait_recv()

    def pstep(step):
        if step == 0:
            for i in range(4):
                p = pages[0, i]
                got = zb[0][p // 16, 1]
                for ch in range(1, NC):
                    got = jnp.where(zc == ch, zb[ch][p // 16, 1], got)
                for half in range(2):
                    lo = half * 2 * CR
                    psel[half, i * CR : (i + 1) * CR] = jnp.where(
                        lax.rem(p, 2) == 0, got[lo : lo + CR], got[lo + CR : lo + 2 * CR]
                    )
            psent(0, psel, ptw, twin)
        if step == 1:
            parrive(0, ptw, twin)
            for i in range(4):
                mine = lax.rem(pages[0, i] // 2, 2) == c
                rows = slice(i * CR, (i + 1) * CR)
                keys_i = jnp.where(mine, psel[0, rows], ptw[0, rows])
                vals_i = jnp.where(mine, psel[1, rows], ptw[1, rows])
                pg[rows] = jnp.where(c == 0, keys_i, vals_i)
            psent(1, pg, pa_l, right)
            psent(2, pg, pa_r, left)
        if step == 2:
            parrive(1, pa_l, right)
            parrive(2, pa_r, left)
            psent(3, pa_l.at[pl.ds(0, PK // 2)], pb_l, right)
            psent(4, pa_r.at[pl.ds(PK // 2, PK // 2)], pb_r, left)
        if step == 3:
            parrive(3, pb_l, right)
            parrive(4, pb_r, left)
            for i in range(4):
                far = lax.rem(lax.rem(pages[0, i] // 4, NX) - x + NX, NX)
                rows = slice(i * CR, (i + 1) * CR)
                opposite = (pb_l if i < 2 else pb_r)[i % 2 * CR : (i % 2 + 1) * CR]
                pcol[zc, rows] = jnp.where(
                    far == 0, pg[rows],
                    jnp.where(far == 3, pa_l[rows], jnp.where(far == 1, pa_r[rows], opposite)),
                )
            psent(5, pcol.at[zc], pcol.at[zc], up)
            psent(6, pcol.at[zc], pcol.at[zc], down)
            psent(7, pcol.at[zc], pcol.at[zc], up2)
            psent(8, pcol.at[zc], pcol2.at[zc], twin)
        if step == 4:
            for slot, to, far in ((5, up, 3), (6, down, 1), (7, up2, 2)):
                row = lax.rem(zc + far, NC)
                parrive(slot, pcol.at[row], to)
                psent(slot + 4, pcol.at[row], pcol2.at[row], twin)
        if step == 5:
            for slot, far in ((8, 0), (9, 3), (10, 1), (11, 2)):
                parrive(slot, pcol2.at[lax.rem(zc + far, NC)], twin)
            for ch in range(NC):
                lo = NC * SK + ch * PK
                kall[lo : lo + PK] = jnp.where(c == 0, pcol[ch], pcol2[ch])
                vall[lo : lo + PK, :128] = jnp.where(c == 0, pcol2[ch], pcol[ch])

    own = NC * 2 * CR
    scale = 128**-0.5 * 1.4426950408889634
    contract = (((1,), (1,)), ((), ()))
    far = NC * KC
    first = [sum(TILES[:t]) for t in range(NT)]

    def spans(t):
        lo, hi = first[t], first[t] + TILES[t]
        return slice(lo, hi), slice(8 * lo, 8 * hi)

    def own_block(t):
        lines, block = spans(t)
        qs[block] = jnp.concatenate([q[lines, h * 128 : (h + 1) * 128] for h in range(8)], 0)
        spot = lax.broadcasted_iota(jnp.int32, (TILES[t], own), 1)
        cols = (spot // CR) % 2 * 128 + spot // (2 * CR) * CR + spot % CR
        line = lax.broadcasted_iota(jnp.int32, (TILES[t], own), 0) + first[t]
        shade = jnp.concatenate([jnp.where(line >= cols, 0.0, NEG)] * 8, 0)
        near[block] = shade + lax.dot_general(
            qs[block], kall[far:], contract, preferred_element_type=jnp.float32
        )

    lane = lax.broadcasted_iota(jnp.int32, (1, NC * KC), 1)
    bias = jnp.zeros((1, NC * KC), jnp.float32)
    for k in range(3):
        here = (lane < NC * SK) & (lane % SK // (2 * CR) == k)
        bias = jnp.where(here & (live[0, k] != 1), NEG, bias)
    for i in range(4):
        shut = False
        for k in range(3):
            d = shift[0, k]
            shut = shut | ((live[0, k] == 1) & (d > s) & (s + 128 - d == pages[0, i] // 2))
        here = (lane >= NC * SK) & ((lane - NC * SK) % PK // CR == i)
        bias = jnp.where(here & shut, NEG, bias)
    for hop in range(8):
        for ch in range(NC):
            zstep(ch, hop)
            if hop >= 5 and (hop - 5) * NC + ch < NT:
                own_block((hop - 5) * NC + ch)
        if hop == 0:
            for cp in local:
                cp.start()
        if hop == 1:
            vall[:, 128:] = jnp.ones((NC * KC + NC * 2 * CR, 128), jnp.bfloat16)
            for ch in range(NC):
                lo = NC * KC + ch * 2 * CR
                kall[lo : lo + 2 * CR] = slab[ch, 0].reshape(2 * CR, 128)
                vall[lo : lo + 2 * CR, :128] = slab[ch, 1].reshape(2 * CR, 128)
        if hop == 4:
            for cp in local:
                cp.wait()
    for ch in range(NC):
        xstep(ch, 0)
    for page, *moves in (
        (0,), (1, (0, 1), (1, 1), (2, 1), (3, 1)), (2, (0, 2), (1, 2)), (3, (2, 2), (3, 2), (0, 3)),
        (4, (1, 3), (2, 3)), (5, (3, 3)),
    ):
        pstep(page)
        for move in moves:
            xstep(*move)

    def ycopy(t, slot):
        lines = pl.ds(first[t], TILES[t])
        view, dst, step = (
            (p2a, hop_l, 1), (p2b, hop_r, 3), (s1b, in_lb, 1), (s3a, in_ra, 3), (s1a, in_la, 1), (s3b, in_rb, 3),
        )[slot]
        return pltpu.make_async_remote_copy(
            src_ref=view.at[lines], dst_ref=dst.at[lines],
            send_sem=ysend.at[t, slot], recv_sem=yrecv.at[t, slot],
            device_id=(s, lax.rem(y + step, 4)), device_id_type=MESH,
        )

    def ysent(t, slot):
        cp = ycopy(t, slot)
        cp.start()
        started.append(cp)

    def relay(t):
        lines, _ = spans(t)
        ycopy(t, 0).wait_recv()
        s1a[lines] = (t1[lines] + hop_l[lines].astype(jnp.float32)).astype(jnp.bfloat16)
        ysent(t, 4)
        ycopy(t, 1).wait_recv()
        s3b[lines] = (t3[lines] + hop_r[lines].astype(jnp.float32)).astype(jnp.bfloat16)
        ysent(t, 5)

    for t in range(NT):
        lines, block = spans(t)
        s1 = lax.dot_general(qs[block], kall[:far], contract, preferred_element_type=jnp.float32)
        s1 = s1 + bias
        s0 = near[block]
        top = jnp.maximum(jnp.max(s0, 1, keepdims=True), jnp.max(s1, 1, keepdims=True))
        e0 = jnp.exp2((s0 - top) * scale).astype(jnp.bfloat16)
        e1 = jnp.exp2((s1 - top) * scale).astype(jnp.bfloat16)
        o = jnp.dot(e1, vall[:far], preferred_element_type=jnp.float32)
        o += jnp.dot(e0, vall[far:], preferred_element_type=jnp.float32)
        o = (o[:, :128] / o[:, 128:]).astype(jnp.bfloat16)
        for h in range(8):
            att[lines, h * 128 : (h + 1) * 128] = o[h * TILES[t] : (h + 1) * TILES[t]]
        a = att[lines]

        def term(step):
            cols_y = pl.ds(pl.multiple_of(lax.rem(y + step, 4) * 512, 512), 512)
            return jnp.dot(a, w[:, cols_y], preferred_element_type=jnp.float32)

        both = term(2).astype(jnp.bfloat16)
        p2a[lines], p2b[lines] = both[:, :256], both[:, 256:]
        ysent(t, 0)
        ysent(t, 1)
        if t:
            relay(t - 1)
        side = term(1)
        t1[lines], s1b[lines] = side[:, :256], side[:, 256:].astype(jnp.bfloat16)
        ysent(t, 2)
        side = term(3)
        s3a[lines], t3[lines] = side[:, :256].astype(jnp.bfloat16), side[:, 256:]
        ysent(t, 3)
        t0[lines] = term(0)
    relay(NT - 1)
    for t in range(NT):
        lines, _ = spans(t)
        for slot in (2, 3, 4, 5):
            ycopy(t, slot).wait_recv()
        for half, ins in ((slice(0, 256), (in_la, in_ra)), (slice(256, 512), (in_lb, in_rb))):
            out[lines, half] = (
                t0[lines, half] + ins[0][lines].astype(jnp.float32) + ins[1][lines].astype(jnp.float32)
            ).astype(jnp.bfloat16)
    for cp in started:
        cp.wait_send()


def call(shift, pages, live, slab, cache, q, w):
    smem = pl.BlockSpec(memory_space=pltpu.SMEM)
    vmem = pl.BlockSpec(memory_space=pltpu.VMEM)
    whole = pl.BlockSpec(memory_space=pl.ANY)
    bf, dma = jnp.bfloat16, pltpu.SemaphoreType.DMA
    rows = q.shape[0]
    keys = NC * KC + NC * 2 * CR

    def many(*shape):
        return [pltpu.VMEM(shape, bf)] * NC

    return pl.pallas_call(
        kernel,
        name="attention",
        out_shape=jax.ShapeDtypeStruct((rows, 512), bf),
        in_specs=[smem, smem, smem, vmem, vmem, whole, whole],
        out_specs=vmem,
        scratch_shapes=many(NZ, 2, 4 * CR, 128)
        + many(2, SK, 128) * 3
        + many(SK, 128) * 7
        + [pltpu.VMEM((2, PK, 128), bf)] * 2
        + [pltpu.VMEM((PK, 128), bf)] * 3
        + [pltpu.VMEM((PK // 2, 128), bf)] * 2
        + [pltpu.VMEM((NC, PK, 128), bf)] * 2
        + [
            pltpu.VMEM(q.shape, bf),
            pltpu.VMEM(w.shape, bf),
            pltpu.VMEM((8 * rows, 128), bf),
            pltpu.VMEM((keys, 128), bf),
            pltpu.VMEM((keys, 256), bf),
            pltpu.VMEM(q.shape, bf),
            pltpu.VMEM((8 * rows, NC * 2 * CR), jnp.float32),
            pltpu.VMEM((rows, 512), jnp.float32),
            pltpu.VMEM((rows, 256), jnp.float32),
            pltpu.VMEM((rows, 256), jnp.float32),
        ]
        + [pltpu.VMEM((rows, 256), bf)] * 12
        + [dma((NC, 2, 8))] * 2 + [dma((NC, 5))] * 2 + [dma((12,))] * 2 + [dma((NT, 6))] * 2 + [dma((2,))],
        compiler_params=pltpu.CompilerParams(
            collective_id=0, has_side_effects=True, vmem_limit_bytes=56 * 2**20
        ),
    )(shift, pages, live, slab, cache, q, w)


def chunked(kv):
    return kv.reshape(2, NC, CR, 2, 128).transpose(1, 3, 0, 2, 4)


def body(queries, keys_values, cache_kv, vertical_pages, slash_shift, slash_live, out_proj):
    return call(
        slash_shift, vertical_pages, slash_live[0], chunked(keys_values), chunked(cache_kv), queries, out_proj
    )


def solution(mesh):
    placed = (
        P("seq", "head"),
        P("seq", None, "head"),
        P("seq", None, "head"),
        P("head", None),
        P("head", None),
        P("seq", "head", None),
        P("head", None),
    )
    return jax.shard_map(
        body, mesh=mesh, in_specs=placed, out_specs=P("seq", "head"), check_vma=False
    )
```

```python
import functools

import jax
import jax.numpy as jnp
from jax import lax
from jax.experimental import pallas as pl
from jax.experimental.pallas import tpu as pltpu
from jax.sharding import PartitionSpec as P

MESH = pl.DeviceIdType.MESH
NC = 4
NZ, NX = 16, 4
TILES = (96, 96, 64)
NT = len(TILES)
CR = 32
KC = 3 * 2 * CR + 4 * CR
NEG = -1e30


def place():
    s = lax.axis_index("seq")
    return s // 8, (s // 2) % NX, s % 2, lax.axis_index("head")


def at(z, x, c, y):
    return (lax.rem(z + NZ, NZ) * 8 + lax.rem(x + NX, NX) * 2 + lax.rem(c + 2, 2), y)


SK = 3 * 2 * CR
PK = 4 * CR


def kernel(shift, pages, live, slab, cache, q_hbm, w_hbm, out, *scratch):
    zb = scratch[:NC]
    sel, tw, my, msg_l, fwd_r, fwd_l, a_l, a_r, b_l, b_r = (
        scratch[NC * (i + 1) : NC * (i + 2)] for i in range(10)
    )
    (psel, ptw, pg, pa_l, pa_r, pa_o, pcol, pcol2,
     q, w, qs, kall, vall, att, near, t0, t1, t3,
     p2a, p2b, s1a, s1b, s3a, s3b, hop_l, hop_r, in_la, in_lb, in_ra, in_rb,
     zsend, zrecv, xsend, xrecv, psend, precv, ysend, yrecv, lsem) = scratch[11 * NC :]
    s = lax.axis_index("seq")
    z, x, c, y = place()
    j = x * 2 + c
    up, down = at(z + 1, x, c, y), at(z - 1, x, c, y)
    right, left = at(z, x + 1, c, y), at(z, x - 1, c, y)
    twin = at(z, x, 1 - c, y)

    bar = pltpu.get_barrier_semaphore()
    others = [(s, lax.rem(y + step, 4)) for step in (1, 3)]
    up2, down2 = at(z + 2, x, c, y), at(z - 2, x, c, y)
    across = at(z, x + 2, c, y)
    for peer in [up, down, down2, right, left, across, twin] + others:
        pl.semaphore_signal(bar, inc=1, device_id=peer, device_id_type=MESH)
    local = [
        pltpu.make_async_copy(q_hbm, q, lsem.at[0]),
        pltpu.make_async_copy(w_hbm, w, lsem.at[1]),
    ]
    for ch in range(NC):
        zb[ch][z, 0] = slab[ch].reshape(4 * CR, 128)
        zb[ch][z, 1] = cache[ch].reshape(4 * CR, 128)
    pl.semaphore_wait(bar, 9)

    started = []

    def zcopy(ch, way, hop, block):
        view = zb[ch].at[block] if hop < 7 else zb[ch].at[block, way]
        return pltpu.make_async_remote_copy(
            src_ref=view, dst_ref=view,
            send_sem=zsend.at[ch, way, hop], recv_sem=zrecv.at[ch, way, hop],
            device_id=up if way == 0 else down, device_id_type=MESH,
        )

    def zarrive(ch, way, hop):
        block = lax.rem(z + NZ - hop - 1, NZ) if way == 0 else lax.rem(z + hop + 1, NZ)
        zcopy(ch, way, hop, block).wait_recv()

    def zstep(ch, hop):
        for way in range(2):
            if hop > 0:
                zarrive(ch, way, hop - 1)
            block = lax.rem(z + NZ - hop, NZ) if way == 0 else lax.rem(z + hop, NZ)
            cp = zcopy(ch, way, hop, block)
            cp.start()
            started.append(cp)

    def xcopy(ch, slot, view, dst, to):
        return pltpu.make_async_remote_copy(
            src_ref=view, dst_ref=dst, send_sem=xsend.at[ch, slot], recv_sem=xrecv.at[ch, slot],
            device_id=to, device_id_type=MESH,
        )

    def send(ch, slot, view, dst, to):
        cp = xcopy(ch, slot, view, dst, to)
        cp.start()
        started.append(cp)

    def arrive(ch, slot, dst, to):
        xcopy(ch, slot, dst, dst, to).wait_recv()

    def turn(k):
        r = lax.rem(shift[0, k], 8)
        swap = lax.rem(r, 2) == 1
        rho = lax.rem(r // 2 + jnp.where(swap & (c == 0), 1, 0), NX)
        return rho, swap

    def xstep(ch, step):
        if step == 0:
            for k in range(3):
                d = shift[0, k]
                m = d // 8 + jnp.where(j + lax.rem(d, 8) >= 8, 1, 0)
                zs = lax.rem(z - m + 2 * NZ, NZ)
                got = zb[ch][zs, jnp.where(z - m >= 0, 0, 1)]
                for half in range(2):
                    sel[ch][half, k * 2 * CR : (k + 1) * 2 * CR] = got[half * 2 * CR : (half + 1) * 2 * CR]
            send(ch, 0, sel[ch], tw[ch], twin)
        if step == 1:
            arrive(ch, 0, tw[ch], twin)
            for k in range(3):
                rho, swap = turn(k)
                rows = slice(k * 2 * CR, (k + 1) * 2 * CR)
                for half in range(2):
                    my[ch][half, rows] = jnp.where(swap, tw[ch][half, rows], sel[ch][half, rows])
                msg_l[ch][rows] = jnp.where(rho == 2, my[ch][1, rows], my[ch][0, rows])
            send(ch, 1, my[ch].at[0], a_l[ch], right)
            send(ch, 2, msg_l[ch], a_r[ch], left)
        if step == 2:
            arrive(ch, 1, a_l[ch], right)
            arrive(ch, 2, a_r[ch], left)
            for k in range(3):
                rho, _ = turn(k)
                rows = slice(k * 2 * CR, (k + 1) * 2 * CR)
                fwd_r[ch][rows] = jnp.where(rho == 2, a_l[ch][rows], my[ch][1, rows])
                fwd_l[ch][rows] = jnp.where(rho == 2, a_r[ch][rows], my[ch][1, rows])
            send(ch, 3, fwd_r[ch], b_l[ch], right)
            send(ch, 4, fwd_l[ch], b_r[ch], left)
        if step == 3:
            arrive(ch, 3, b_l[ch], right)
            arrive(ch, 4, b_r[ch], left)
            for k in range(3):
                rho, _ = turn(k)
                rows = slice(k * 2 * CR, (k + 1) * 2 * CR)
                lo = ch * SK + k * 2 * CR
                kall[lo : lo + 2 * CR] = jnp.where(
                    rho == 0, my[ch][0, rows],
                    jnp.where(rho == 1, a_l[ch][rows], jnp.where(rho == 2, b_l[ch][rows], a_r[ch][rows])),
                )
                vall[lo : lo + 2 * CR, :128] = jnp.where(
                    rho == 0, my[ch][1, rows], jnp.where(rho == 1, b_l[ch][rows], b_r[ch][rows])
                )

    zc = lax.rem(z, NC)

    def pcopy(slot, view, dst, to):
        return pltpu.make_async_remote_copy(
            src_ref=view, dst_ref=dst, send_sem=psend.at[slot], recv_sem=precv.at[slot],
            device_id=to, device_id_type=MESH,
        )

    def psent(slot, view, dst, to):
        cp = pcopy(slot, view, dst, to)
        cp.start()
        started.append(cp)

    def parrive(slot, dst, to):
        pcopy(slot, dst, dst, to).wait_recv()

    def pstep(step):
        if step == 0:
            for i in range(4):
                p = pages[0, i]
                got = zb[0][p // 16, 1]
                for ch in range(1, NC):
                    got = jnp.where(zc == ch, zb[ch][p // 16, 1], got)
                for half in range(2):
                    lo = half * 2 * CR
                    psel[half, i * CR : (i + 1) * CR] = jnp.where(
                        lax.rem(p, 2) == 0, got[lo : lo + CR], got[lo + CR : lo + 2 * CR]
                    )
            psent(0, psel, ptw, twin)
        if step == 1:
            parrive(0, ptw, twin)
            for i in range(4):
                mine = lax.rem(pages[0, i] // 2, 2) == c
                rows = slice(i * CR, (i + 1) * CR)
                keys_i = jnp.where(mine, psel[0, rows], ptw[0, rows])
                vals_i = jnp.where(mine, psel[1, rows], ptw[1, rows])
                pg[rows] = jnp.where(c == 0, keys_i, vals_i)
            psent(1, pg, pa_l, right)
            psent(2, pg, pa_r, left)
            psent(3, pg, pa_o, across)
        if step == 2:
            parrive(1, pa_l, right)
            parrive(2, pa_r, left)
            parrive(3, pa_o, across)
            for i in range(4):
                far = lax.rem(lax.rem(pages[0, i] // 4, NX) - x + NX, NX)
                rows = slice(i * CR, (i + 1) * CR)
                pcol[zc, rows] = jnp.where(
                    far == 0, pg[rows],
                    jnp.where(far == 3, pa_l[rows], jnp.where(far == 1, pa_r[rows], pa_o[rows])),
                )
            psent(5, pcol.at[zc], pcol.at[zc], up)
            psent(6, pcol.at[zc], pcol.at[zc], down)
            psent(7, pcol.at[zc], pcol.at[zc], up2)
            psent(8, pcol.at[zc], pcol2.at[zc], twin)
        if step == 3:
            for slot, to, far in ((5, up, 3), (6, down, 1), (7, up2, 2)):
                row = lax.rem(zc + far, NC)
                parrive(slot, pcol.at[row], to)
                psent(slot + 4, pcol.at[row], pcol2.at[row], twin)
        if step == 4:
            for slot, far in ((8, 0), (9, 3), (10, 1), (11, 2)):
                parrive(slot, pcol2.at[lax.rem(zc + far, NC)], twin)
            for ch in range(NC):
                lo = NC * SK + ch * PK
                kall[lo : lo + PK] = jnp.where(c == 0, pcol[ch], pcol2[ch])
                vall[lo : lo + PK, :128] = jnp.where(c == 0, pcol2[ch], pcol[ch])

    own = NC * 2 * CR
    scale = 128**-0.5 * 1.4426950408889634
    contract = (((1,), (1,)), ((), ()))
    far = NC * KC
    first = [sum(TILES[:t]) for t in range(NT)]

    def spans(t):
        lo, hi = first[t], first[t] + TILES[t]
        return slice(lo, hi), slice(8 * lo, 8 * hi)

    def own_block(t):
        lines, block = spans(t)
        qs[block] = jnp.concatenate([q[lines, h * 128 : (h + 1) * 128] for h in range(8)], 0)
        spot = lax.broadcasted_iota(jnp.int32, (TILES[t], own), 1)
        cols = (spot // CR) % 2 * 128 + spot // (2 * CR) * CR + spot % CR
        line = lax.broadcasted_iota(jnp.int32, (TILES[t], own), 0) + first[t]
        shade = jnp.concatenate([jnp.where(line >= cols, 0.0, NEG)] * 8, 0)
        near[block] = shade + lax.dot_general(
            qs[block], kall[far:], contract, preferred_element_type=jnp.float32
        )

    lane = lax.broadcasted_iota(jnp.int32, (1, NC * KC), 1)
    bias = jnp.zeros((1, NC * KC), jnp.float32)
    for k in range(3):
        here = (lane < NC * SK) & (lane % SK // (2 * CR) == k)
        bias = jnp.where(here & (live[0, k] != 1), NEG, bias)
    for i in range(4):
        shut = False
        for k in range(3):
            d = shift[0, k]
            shut = shut | ((live[0, k] == 1) & (d > s) & (s + 128 - d == pages[0, i] // 2))
        here = (lane >= NC * SK) & ((lane - NC * SK) % PK // CR == i)
        bias = jnp.where(here & shut, NEG, bias)
    for hop in range(8):
        for ch in range(NC):
            zstep(ch, hop)
            if hop >= 5 and (hop - 5) * NC + ch < NT:
                own_block((hop - 5) * NC + ch)
        if hop == 0:
            for cp in local:
                cp.start()
        if hop == 1:
            vall[:, 128:] = jnp.ones((NC * KC + NC * 2 * CR, 128), jnp.bfloat16)
            for ch in range(NC):
                lo = NC * KC + ch * 2 * CR
                kall[lo : lo + 2 * CR] = slab[ch, 0].reshape(2 * CR, 128)
                vall[lo : lo + 2 * CR, :128] = slab[ch, 1].reshape(2 * CR, 128)
        if hop == 4:
            for cp in local:
                cp.wait()
    for ch in range(NC):
        for way in range(2):
            zarrive(ch, way, 7)
    for page, *moves in (
        (0, (0, 0), (1, 0), (2, 0), (3, 0)), (1, (0, 1), (1, 1), (2, 1), (3, 1), (0, 2)),
        (2, (1, 2), (2, 2), (3, 2)), (3, (0, 3), (1, 3), (2, 3)), (4, (3, 3)),
    ):
        pstep(page)
        for move in moves:
            xstep(*move)

    def ycopy(t, slot):
        lines = pl.ds(first[t], TILES[t])
        view, dst, step = (
            (p2a, hop_l, 1), (p2b, hop_r, 3), (s1b, in_lb, 1), (s3a, in_ra, 3), (s1a, in_la, 1), (s3b, in_rb, 3),
        )[slot]
        return pltpu.make_async_remote_copy(
            src_ref=view.at[lines], dst_ref=dst.at[lines],
            send_sem=ysend.at[t, slot], recv_sem=yrecv.at[t, slot],
            device_id=(s, lax.rem(y + step, 4)), device_id_type=MESH,
        )

    def ysent(t, slot):
        cp = ycopy(t, slot)
        cp.start()
        started.append(cp)

    def relay(t):
        lines, _ = spans(t)
        ycopy(t, 0).wait_recv()
        s1a[lines] = (t1[lines] + hop_l[lines].astype(jnp.float32)).astype(jnp.bfloat16)
        ysent(t, 4)
        ycopy(t, 1).wait_recv()
        s3b[lines] = (t3[lines] + hop_r[lines].astype(jnp.float32)).astype(jnp.bfloat16)
        ysent(t, 5)

    for t in range(NT):
        lines, block = spans(t)
        s1 = lax.dot_general(qs[block], kall[:far], contract, preferred_element_type=jnp.float32)
        s1 = s1 + bias
        s0 = near[block]
        top = jnp.maximum(jnp.max(s0, 1, keepdims=True), jnp.max(s1, 1, keepdims=True))
        e0 = jnp.exp2((s0 - top) * scale).astype(jnp.bfloat16)
        e1 = jnp.exp2((s1 - top) * scale).astype(jnp.bfloat16)
        o = jnp.dot(e1, vall[:far], preferred_element_type=jnp.float32)
        o += jnp.dot(e0, vall[far:], preferred_element_type=jnp.float32)
        o = (o[:, :128] / o[:, 128:]).astype(jnp.bfloat16)
        for h in range(8):
            att[lines, h * 128 : (h + 1) * 128] = o[h * TILES[t] : (h + 1) * TILES[t]]
        a = att[lines]

        def term(step):
            cols_y = pl.ds(pl.multiple_of(lax.rem(y + step, 4) * 512, 512), 512)
            return jnp.dot(a, w[:, cols_y], preferred_element_type=jnp.float32)

        both = term(2).astype(jnp.bfloat16)
        p2a[lines], p2b[lines] = both[:, :256], both[:, 256:]
        ysent(t, 0)
        ysent(t, 1)
        if t:
            relay(t - 1)
        side = term(1)
        t1[lines], s1b[lines] = side[:, :256], side[:, 256:].astype(jnp.bfloat16)
        ysent(t, 2)
        side = term(3)
        s3a[lines], t3[lines] = side[:, :256].astype(jnp.bfloat16), side[:, 256:]
        ysent(t, 3)
        t0[lines] = term(0)
    relay(NT - 1)
    for t in range(NT):
        lines, _ = spans(t)
        for slot in (2, 3, 4, 5):
            ycopy(t, slot).wait_recv()
        for half, ins in ((slice(0, 256), (in_la, in_ra)), (slice(256, 512), (in_lb, in_rb))):
            out[lines, half] = (
                t0[lines, half] + ins[0][lines].astype(jnp.float32) + ins[1][lines].astype(jnp.float32)
            ).astype(jnp.bfloat16)
    for cp in started:
        cp.wait_send()


def call(shift, pages, live, slab, cache, q, w):
    smem = pl.BlockSpec(memory_space=pltpu.SMEM)
    vmem = pl.BlockSpec(memory_space=pltpu.VMEM)
    whole = pl.BlockSpec(memory_space=pl.ANY)
    bf, dma = jnp.bfloat16, pltpu.SemaphoreType.DMA
    rows = q.shape[0]
    keys = NC * KC + NC * 2 * CR

    def many(*shape):
        return [pltpu.VMEM(shape, bf)] * NC

    return pl.pallas_call(
        kernel,
        name="attention",
        out_shape=jax.ShapeDtypeStruct((rows, 512), bf),
        in_specs=[smem, smem, smem, vmem, vmem, whole, whole],
        out_specs=vmem,
        scratch_shapes=many(NZ, 2, 4 * CR, 128)
        + many(2, SK, 128) * 3
        + many(SK, 128) * 7
        + [pltpu.VMEM((2, PK, 128), bf)] * 2
        + [pltpu.VMEM((PK, 128), bf)] * 4
        + [pltpu.VMEM((NC, PK, 128), bf)] * 2
        + [
            pltpu.VMEM(q.shape, bf),
            pltpu.VMEM(w.shape, bf),
            pltpu.VMEM((8 * rows, 128), bf),
            pltpu.VMEM((keys, 128), bf),
            pltpu.VMEM((keys, 256), bf),
            pltpu.VMEM(q.shape, bf),
            pltpu.VMEM((8 * rows, NC * 2 * CR), jnp.float32),
            pltpu.VMEM((rows, 512), jnp.float32),
            pltpu.VMEM((rows, 256), jnp.float32),
            pltpu.VMEM((rows, 256), jnp.float32),
        ]
        + [pltpu.VMEM((rows, 256), bf)] * 12
        + [dma((NC, 2, 8))] * 2 + [dma((NC, 5))] * 2 + [dma((12,))] * 2 + [dma((NT, 6))] * 2 + [dma((2,))],
        compiler_params=pltpu.CompilerParams(
            collective_id=0, has_side_effects=True, vmem_limit_bytes=56 * 2**20
        ),
    )(shift, pages, live, slab, cache, q, w)


def chunked(kv):
    return kv.reshape(2, NC, CR, 2, 128).transpose(1, 3, 0, 2, 4)


def body(queries, keys_values, cache_kv, vertical_pages, slash_shift, slash_live, out_proj):
    return call(
        slash_shift, vertical_pages, slash_live[0], chunked(keys_values), chunked(cache_kv), queries, out_proj
    )


def solution(mesh):
    placed = (
        P("seq", "head"),
        P("seq", None, "head"),
        P("seq", None, "head"),
        P("head", None),
        P("head", None),
        P("seq", "head", None),
        P("head", None),
    )
    return jax.shard_map(
        body, mesh=mesh, in_specs=placed, out_specs=P("seq", "head"), check_vma=False
    )
```

```python
import functools

import jax
import jax.numpy as jnp
from jax import lax
from jax.experimental import pallas as pl
from jax.experimental.pallas import tpu as pltpu
from jax.sharding import PartitionSpec as P

MESH = pl.DeviceIdType.MESH
NC = 4
NZ, NX = 16, 4
TILES = (112, 96, 48)
NT = len(TILES)
CR = 32
KC = 3 * 2 * CR + 4 * CR
NEG = -1e30


def place():
    s = lax.axis_index("seq")
    return s // 8, (s // 2) % NX, s % 2, lax.axis_index("head")


def at(z, x, c, y):
    return (lax.rem(z + NZ, NZ) * 8 + lax.rem(x + NX, NX) * 2 + lax.rem(c + 2, 2), y)


SK = 3 * 2 * CR
PK = 4 * CR


def kernel(shift, pages, live, slab, cache, q_hbm, w_hbm, out, *scratch):
    zb = scratch[:NC]
    sel, tw, my, msg_l, fwd_r, fwd_l, a_l, a_r, b_l, b_r = (
        scratch[NC * (i + 1) : NC * (i + 2)] for i in range(10)
    )
    (psel, ptw, pg, pa_l, pa_r, pa_o, pcol, pcol2,
     q, w, qs, kall, vall, att, near, t0, t1, t3,
     p2a, p2b, s1a, s1b, s3a, s3b, hop_l, hop_r, in_la, in_lb, in_ra, in_rb,
     zsend, zrecv, xsend, xrecv, psend, precv, ysend, yrecv, lsem) = scratch[11 * NC :]
    s = lax.axis_index("seq")
    z, x, c, y = place()
    j = x * 2 + c
    up, down = at(z + 1, x, c, y), at(z - 1, x, c, y)
    right, left = at(z, x + 1, c, y), at(z, x - 1, c, y)
    twin = at(z, x, 1 - c, y)

    bar = pltpu.get_barrier_semaphore()
    others = [(s, lax.rem(y + step, 4)) for step in (1, 3)]
    up2, down2 = at(z + 2, x, c, y), at(z - 2, x, c, y)
    across = at(z, x + 2, c, y)
    for peer in [up, down, down2, right, left, across, twin] + others:
        pl.semaphore_signal(bar, inc=1, device_id=peer, device_id_type=MESH)
    local = [
        pltpu.make_async_copy(q_hbm, q, lsem.at[0]),
        pltpu.make_async_copy(w_hbm, w, lsem.at[1]),
    ]
    for ch in range(NC):
        zb[ch][z, 0] = slab[ch].reshape(4 * CR, 128)
        zb[ch][z, 1] = cache[ch].reshape(4 * CR, 128)
    pl.semaphore_wait(bar, 9)

    started = []

    def zcopy(ch, way, hop, block):
        view = zb[ch].at[block] if hop < 7 else zb[ch].at[block, way]
        return pltpu.make_async_remote_copy(
            src_ref=view, dst_ref=view,
            send_sem=zsend.at[ch, way, hop], recv_sem=zrecv.at[ch, way, hop],
            device_id=up if way == 0 else down, device_id_type=MESH,
        )

    def zarrive(ch, way, hop):
        block = lax.rem(z + NZ - hop - 1, NZ) if way == 0 else lax.rem(z + hop + 1, NZ)
        zcopy(ch, way, hop, block).wait_recv()

    def zstep(ch, hop):
        for way in range(2):
            if hop > 0:
                zarrive(ch, way, hop - 1)
            block = lax.rem(z + NZ - hop, NZ) if way == 0 else lax.rem(z + hop, NZ)
            cp = zcopy(ch, way, hop, block)
            cp.start()
            started.append(cp)

    def xcopy(ch, slot, view, dst, to):
        return pltpu.make_async_remote_copy(
            src_ref=view, dst_ref=dst, send_sem=xsend.at[ch, slot], recv_sem=xrecv.at[ch, slot],
            device_id=to, device_id_type=MESH,
        )

    def send(ch, slot, view, dst, to):
        cp = xcopy(ch, slot, view, dst, to)
        cp.start()
        started.append(cp)

    def arrive(ch, slot, dst, to):
        xcopy(ch, slot, dst, dst, to).wait_recv()

    def turn(k):
        r = lax.rem(shift[0, k], 8)
        swap = lax.rem(r, 2) == 1
        rho = lax.rem(r // 2 + jnp.where(swap & (c == 0), 1, 0), NX)
        return rho, swap

    def xstep(ch, step):
        if step == 0:
            for k in range(3):
                d = shift[0, k]
                m = d // 8 + jnp.where(j + lax.rem(d, 8) >= 8, 1, 0)
                zs = lax.rem(z - m + 2 * NZ, NZ)
                got = zb[ch][zs, jnp.where(z - m >= 0, 0, 1)]
                for half in range(2):
                    sel[ch][half, k * 2 * CR : (k + 1) * 2 * CR] = got[half * 2 * CR : (half + 1) * 2 * CR]
            send(ch, 0, sel[ch], tw[ch], twin)
        if step == 1:
            arrive(ch, 0, tw[ch], twin)
            for k in range(3):
                rho, swap = turn(k)
                rows = slice(k * 2 * CR, (k + 1) * 2 * CR)
                for half in range(2):
                    my[ch][half, rows] = jnp.where(swap, tw[ch][half, rows], sel[ch][half, rows])
                msg_l[ch][rows] = jnp.where(rho == 2, my[ch][1, rows], my[ch][0, rows])
            send(ch, 1, my[ch].at[0], a_l[ch], right)
            send(ch, 2, msg_l[ch], a_r[ch], left)
        if step == 2:
            arrive(ch, 1, a_l[ch], right)
            arrive(ch, 2, a_r[ch], left)
            for k in range(3):
                rho, _ = turn(k)
                rows = slice(k * 2 * CR, (k + 1) * 2 * CR)
                fwd_r[ch][rows] = jnp.where(rho == 2, a_l[ch][rows], my[ch][1, rows])
                fwd_l[ch][rows] = jnp.where(rho == 2, a_r[ch][rows], my[ch][1, rows])
            send(ch, 3, fwd_r[ch], b_l[ch], right)
            send(ch, 4, fwd_l[ch], b_r[ch], left)
        if step == 3:
            arrive(ch, 3, b_l[ch], right)
            arrive(ch, 4, b_r[ch], left)
            for k in range(3):
                rho, _ = turn(k)
                rows = slice(k * 2 * CR, (k + 1) * 2 * CR)
                lo = ch * SK + k * 2 * CR
                kall[lo : lo + 2 * CR] = jnp.where(
                    rho == 0, my[ch][0, rows],
                    jnp.where(rho == 1, a_l[ch][rows], jnp.where(rho == 2, b_l[ch][rows], a_r[ch][rows])),
                )
                vall[lo : lo + 2 * CR, :128] = jnp.where(
                    rho == 0, my[ch][1, rows], jnp.where(rho == 1, b_l[ch][rows], b_r[ch][rows])
                )

    zc = lax.rem(z, NC)

    def pcopy(slot, view, dst, to):
        return pltpu.make_async_remote_copy(
            src_ref=view, dst_ref=dst, send_sem=psend.at[slot], recv_sem=precv.at[slot],
            device_id=to, device_id_type=MESH,
        )

    def psent(slot, view, dst, to):
        cp = pcopy(slot, view, dst, to)
        cp.start()
        started.append(cp)

    def parrive(slot, dst, to):
        pcopy(slot, dst, dst, to).wait_recv()

    def pstep(step):
        if step == 0:
            for i in range(4):
                p = pages[0, i]
                got = zb[0][p // 16, 1]
                for ch in range(1, NC):
                    got = jnp.where(zc == ch, zb[ch][p // 16, 1], got)
                for half in range(2):
                    lo = half * 2 * CR
                    psel[half, i * CR : (i + 1) * CR] = jnp.where(
                        lax.rem(p, 2) == 0, got[lo : lo + CR], got[lo + CR : lo + 2 * CR]
                    )
            psent(0, psel, ptw, twin)
        if step == 1:
            parrive(0, ptw, twin)
            for i in range(4):
                mine = lax.rem(pages[0, i] // 2, 2) == c
                rows = slice(i * CR, (i + 1) * CR)
                keys_i = jnp.where(mine, psel[0, rows], ptw[0, rows])
                vals_i = jnp.where(mine, psel[1, rows], ptw[1, rows])
                pg[rows] = jnp.where(c == 0, keys_i, vals_i)
            psent(1, pg, pa_l, right)
            psent(2, pg, pa_r, left)
            psent(3, pg, pa_o, across)
        if step == 2:
            parrive(1, pa_l, right)
            parrive(2, pa_r, left)
            parrive(3, pa_o, across)
            for i in range(4):
                far = lax.rem(lax.rem(pages[0, i] // 4, NX) - x + NX, NX)
                rows = slice(i * CR, (i + 1) * CR)
                pcol[zc, rows] = jnp.where(
                    far == 0, pg[rows],
                    jnp.where(far == 3, pa_l[rows], jnp.where(far == 1, pa_r[rows], pa_o[rows])),
                )
            psent(5, pcol.at[zc], pcol.at[zc], up)
            psent(6, pcol.at[zc], pcol.at[zc], down)
            psent(7, pcol.at[zc], pcol.at[zc], up2)
            psent(8, pcol.at[zc], pcol2.at[zc], twin)
        if step == 3:
            for slot, to, far in ((5, up, 3), (6, down, 1), (7, up2, 2)):
                row = lax.rem(zc + far, NC)
                parrive(slot, pcol.at[row], to)
                psent(slot + 4, pcol.at[row], pcol2.at[row], twin)
        if step == 4:
            for slot, far in ((8, 0), (9, 3), (10, 1), (11, 2)):
                parrive(slot, pcol2.at[lax.rem(zc + far, NC)], twin)
            for ch in range(NC):
                lo = NC * SK + ch * PK
                kall[lo : lo + PK] = jnp.where(c == 0, pcol[ch], pcol2[ch])
                vall[lo : lo + PK, :128] = jnp.where(c == 0, pcol2[ch], pcol[ch])

    own = NC * 2 * CR
    scale = 128**-0.5 * 1.4426950408889634
    contract = (((1,), (1,)), ((), ()))
    far = NC * KC
    first = [sum(TILES[:t]) for t in range(NT)]

    def spans(t):
        lo, hi = first[t], first[t] + TILES[t]
        return slice(lo, hi), slice(8 * lo, 8 * hi)

    def own_block(t):
        lines, block = spans(t)
        qs[block] = jnp.concatenate([q[lines, h * 128 : (h + 1) * 128] for h in range(8)], 0)
        spot = lax.broadcasted_iota(jnp.int32, (TILES[t], own), 1)
        cols = (spot // CR) % 2 * 128 + spot // (2 * CR) * CR + spot % CR
        line = lax.broadcasted_iota(jnp.int32, (TILES[t], own), 0) + first[t]
        shade = jnp.concatenate([jnp.where(line >= cols, 0.0, NEG)] * 8, 0)
        near[block] = shade + lax.dot_general(
            qs[block], kall[far:], contract, preferred_element_type=jnp.float32
        )

    lane = lax.broadcasted_iota(jnp.int32, (1, NC * KC), 1)
    bias = jnp.zeros((1, NC * KC), jnp.float32)
    for k in range(3):
        here = (lane < NC * SK) & (lane % SK // (2 * CR) == k)
        bias = jnp.where(here & (live[0, k] != 1), NEG, bias)
    for i in range(4):
        shut = False
        for k in range(3):
            d = shift[0, k]
            shut = shut | ((live[0, k] == 1) & (d > s) & (s + 128 - d == pages[0, i] // 2))
        here = (lane >= NC * SK) & ((lane - NC * SK) % PK // CR == i)
        bias = jnp.where(here & shut, NEG, bias)
    for hop in range(8):
        for ch in range(NC):
            zstep(ch, hop)
            if hop >= 5 and (hop - 5) * NC + ch < NT:
                own_block((hop - 5) * NC + ch)
        if hop == 0:
            for cp in local:
                cp.start()
        if hop == 1:
            vall[:, 128:] = jnp.ones((NC * KC + NC * 2 * CR, 128), jnp.bfloat16)
            for ch in range(NC):
                lo = NC * KC + ch * 2 * CR
                kall[lo : lo + 2 * CR] = slab[ch, 0].reshape(2 * CR, 128)
                vall[lo : lo + 2 * CR, :128] = slab[ch, 1].reshape(2 * CR, 128)
        if hop == 4:
            for cp in local:
                cp.wait()
    for ch in range(NC):
        for way in range(2):
            zarrive(ch, way, 7)
    for page, *moves in (
        (0, (0, 0), (1, 0), (2, 0), (3, 0)), (1, (0, 1), (1, 1), (2, 1), (3, 1), (0, 2)),
        (2, (1, 2), (2, 2), (3, 2)), (3, (0, 3), (1, 3), (2, 3)), (4, (3, 3)),
    ):
        pstep(page)
        for move in moves:
            xstep(*move)

    def ycopy(t, slot):
        lines = pl.ds(first[t], TILES[t])
        view, dst, step = (
            (p2a, hop_l, 1), (p2b, hop_r, 3), (s1b, in_lb, 1), (s3a, in_ra, 3), (s1a, in_la, 1), (s3b, in_rb, 3),
        )[slot]
        return pltpu.make_async_remote_copy(
            src_ref=view.at[lines], dst_ref=dst.at[lines],
            send_sem=ysend.at[t, slot], recv_sem=yrecv.at[t, slot],
            device_id=(s, lax.rem(y + step, 4)), device_id_type=MESH,
        )

    def ysent(t, slot):
        cp = ycopy(t, slot)
        cp.start()
        started.append(cp)

    def relay(t):
        lines, _ = spans(t)
        ycopy(t, 0).wait_recv()
        s1a[lines] = (t1[lines] + hop_l[lines].astype(jnp.float32)).astype(jnp.bfloat16)
        ysent(t, 4)
        ycopy(t, 1).wait_recv()
        s3b[lines] = (t3[lines] + hop_r[lines].astype(jnp.float32)).astype(jnp.bfloat16)
        ysent(t, 5)

    for t in range(NT):
        lines, block = spans(t)
        s1 = lax.dot_general(qs[block], kall[:far], contract, preferred_element_type=jnp.float32)
        s1 = s1 + bias
        s0 = near[block]
        top = jnp.maximum(jnp.max(s0, 1, keepdims=True), jnp.max(s1, 1, keepdims=True))
        e0 = jnp.exp2((s0 - top) * scale).astype(jnp.bfloat16)
        e1 = jnp.exp2((s1 - top) * scale).astype(jnp.bfloat16)
        o = jnp.dot(e1, vall[:far], preferred_element_type=jnp.float32)
        o += jnp.dot(e0, vall[far:], preferred_element_type=jnp.float32)
        o = (o[:, :128] / o[:, 128:]).astype(jnp.bfloat16)
        for h in range(8):
            att[lines, h * 128 : (h + 1) * 128] = o[h * TILES[t] : (h + 1) * TILES[t]]
        a = att[lines]

        def term(step):
            cols_y = pl.ds(pl.multiple_of(lax.rem(y + step, 4) * 512, 512), 512)
            return jnp.dot(a, w[:, cols_y], preferred_element_type=jnp.float32)

        both = term(2).astype(jnp.bfloat16)
        p2a[lines], p2b[lines] = both[:, :256], both[:, 256:]
        ysent(t, 0)
        ysent(t, 1)
        if t:
            relay(t - 1)
        side = term(1)
        t1[lines], s1b[lines] = side[:, :256], side[:, 256:].astype(jnp.bfloat16)
        ysent(t, 2)
        side = term(3)
        s3a[lines], t3[lines] = side[:, :256].astype(jnp.bfloat16), side[:, 256:]
        ysent(t, 3)
        t0[lines] = term(0)
    for t in range(NT):
        lines, _ = spans(t)
        if t == 1:
            relay(NT - 1)
        for slot in (2, 3, 4, 5):
            ycopy(t, slot).wait_recv()
        for half, ins in ((slice(0, 256), (in_la, in_ra)), (slice(256, 512), (in_lb, in_rb))):
            out[lines, half] = (
                t0[lines, half] + ins[0][lines].astype(jnp.float32) + ins[1][lines].astype(jnp.float32)
            ).astype(jnp.bfloat16)
    for cp in started:
        cp.wait_send()


def call(shift, pages, live, slab, cache, q, w):
    smem = pl.BlockSpec(memory_space=pltpu.SMEM)
    vmem = pl.BlockSpec(memory_space=pltpu.VMEM)
    whole = pl.BlockSpec(memory_space=pl.ANY)
    bf, dma = jnp.bfloat16, pltpu.SemaphoreType.DMA
    rows = q.shape[0]
    keys = NC * KC + NC * 2 * CR

    def many(*shape):
        return [pltpu.VMEM(shape, bf)] * NC

    return pl.pallas_call(
        kernel,
        name="attention",
        out_shape=jax.ShapeDtypeStruct((rows, 512), bf),
        in_specs=[smem, smem, smem, vmem, vmem, whole, whole],
        out_specs=vmem,
        scratch_shapes=many(NZ, 2, 4 * CR, 128)
        + many(2, SK, 128) * 3
        + many(SK, 128) * 7
        + [pltpu.VMEM((2, PK, 128), bf)] * 2
        + [pltpu.VMEM((PK, 128), bf)] * 4
        + [pltpu.VMEM((NC, PK, 128), bf)] * 2
        + [
            pltpu.VMEM(q.shape, bf),
            pltpu.VMEM(w.shape, bf),
            pltpu.VMEM((8 * rows, 128), bf),
            pltpu.VMEM((keys, 128), bf),
            pltpu.VMEM((keys, 256), bf),
            pltpu.VMEM(q.shape, bf),
            pltpu.VMEM((8 * rows, NC * 2 * CR), jnp.float32),
            pltpu.VMEM((rows, 512), jnp.float32),
            pltpu.VMEM((rows, 256), jnp.float32),
            pltpu.VMEM((rows, 256), jnp.float32),
        ]
        + [pltpu.VMEM((rows, 256), bf)] * 12
        + [dma((NC, 2, 8))] * 2 + [dma((NC, 5))] * 2 + [dma((12,))] * 2 + [dma((NT, 6))] * 2 + [dma((2,))],
        compiler_params=pltpu.CompilerParams(
            collective_id=0, has_side_effects=True, vmem_limit_bytes=56 * 2**20
        ),
    )(shift, pages, live, slab, cache, q, w)


def chunked(kv):
    return kv.reshape(2, NC, CR, 2, 128).transpose(1, 3, 0, 2, 4)


def body(queries, keys_values, cache_kv, vertical_pages, slash_shift, slash_live, out_proj):
    return call(
        slash_shift, vertical_pages, slash_live[0], chunked(keys_values), chunked(cache_kv), queries, out_proj
    )


def solution(mesh):
    placed = (
        P("seq", "head"),
        P("seq", None, "head"),
        P("seq", None, "head"),
        P("head", None),
        P("head", None),
        P("seq", "head", None),
        P("head", None),
    )
    return jax.shard_map(
        body, mesh=mesh, in_specs=placed, out_specs=P("seq", "head"), check_vma=False
    )
```
